32 devices in a mesh: region: 2 (over y), snp: 8 (over z, x), sample: 2 (over core).
Axes of the slice: x: 2, y: 2, z: 4, core: 2. Of those that a mesh axis runs over, the one named last changes fastest.
Arguments:
- dosage: bfloat16 [4096, 24576], P('sample', ('region', 'snp')), parts along dimension 1, as said below
- partners: int32 [48, 3], P(('region', 'snp')), parts along dimension 0, may hold values from -1 to 23, as said below
Outputs:
- ld_tiles: float32 [48, 3, 512, 512], P(('region', 'snp'), None, 'sample'), parts along dimension 0
The draws below stay inside these ranges and needn't reach their ends.
There are 2 independent parts, one for each index of `region`. The reference program is written for one: setup_inputs(seed, part) draws one part's arguments, and reference() takes and returns one part's arrays. A program takes and returns all parts, laid end to end along the dimension named above; each array names one. Nothing has to cross between parts.
Inputs may be any that keep to these rules, and one draw needn't show every extreme that they name: For each block b: partners[b, 0] = b; the other entries are distinct blocks b + 1 to b + 2 in rising order, followed by -1 entries only; block 0 lists all 3 blocks 0 to 2. `dosage`: dosages are real values within 0 and 2.
All inputs are finite; a program needn't handle non-finite values.
Results may differ from the reference program's by a relative error of at most 0.0013.
Values may be sent and summed in bfloat16 or wider, within the bound.
A program may use at most 128 MiB of HBM per device.

```python
import jax
import jax.numpy as jnp
from jax import lax

BLOCK = 512
REACH = 2
KMAX = 3
NBLK = 24
SNPS = 12288
SAMPLES = 4096


def draw_dosage(key, part):
    key = jax.random.fold_in(key, 11)
    keys = jax.random.split(key, 5)
    low = jnp.log(0.03)
    high = jnp.log(0.5)
    first = jnp.exp(jax.random.uniform(keys[0], (1, SNPS), jnp.float32, low, high))
    second = jnp.exp(jax.random.uniform(keys[1], (1, SNPS), jnp.float32, low, high))
    rows = jnp.arange(SAMPLES, dtype=jnp.int32)[:, None]
    freq = jnp.where(rows < SAMPLES // 2, first, second)
    latent = jax.random.normal(keys[2], (SAMPLES, 1), jnp.float32)
    loading = jax.random.uniform(keys[3], (1, SNPS), jnp.float32, -0.6, 0.6)
    noise = jax.random.normal(keys[4], (SAMPLES, SNPS), jnp.float32)
    mixed = loading * latent + jnp.sqrt(1.0 - loading * loading) * noise
    value = 2.0 * freq + jnp.sqrt(2.0 * freq * (1.0 - freq)) * mixed
    return jnp.clip(value, 0.0, 2.0).astype(jnp.bfloat16)


def draw_partners(key, part):
    key = jax.random.fold_in(key, 5)
    include = jax.random.randint(key, (NBLK, REACH), 0, 2).astype(jnp.int32)
    blocks = jnp.arange(NBLK, dtype=jnp.int32)[:, None]
    offsets = jnp.arange(1, REACH + 1, dtype=jnp.int32)[None, :]
    include = jnp.where(blocks == 0, 1, include)
    include = jnp.where(blocks + offsets < NBLK, include, 0)
    position = jnp.cumsum(include, axis=1)
    columns = [blocks[:, 0]]
    for slot in range(1, KMAX):
        hit = (include == 1) & (position == slot)
        found = jnp.sum(jnp.where(hit, blocks + offsets + 1, 0), axis=1)
        columns.append(found - 1)
    return jnp.stack(columns, axis=1).astype(jnp.int32)


def setup_inputs(seed: int = 0, part: int = 0) -> dict:
    splits = jax.random.split(jax.random.key(seed), 3)
    part_splits = jax.random.split(jax.random.fold_in(splits[2], part), 3)
    dosage = draw_dosage(jax.random.fold_in(jax.random.fold_in(splits[2], part), 71), part)
    partners = draw_partners(jax.random.fold_in(jax.random.fold_in(splits[2], part), 71), part)
    return {"dosage": dosage, "partners": partners}


def reference(dosage, partners):
    values = dosage.astype(jnp.float32)
    total = lax.optimization_barrier(jnp.sum(values, axis=0))
    square_total = lax.optimization_barrier(jnp.sum(values * values, axis=0))
    mean = total / SAMPLES
    variance = square_total / SAMPLES - mean * mean
    scale = lax.rsqrt(variance + 1e-05)
    standard = ((values - mean[None, :]) * scale[None, :]).astype(jnp.bfloat16)

    def one_block(index):
        own = lax.dynamic_slice_in_dim(standard, index * BLOCK, BLOCK, 1)
        tiles = []
        for slot in range(KMAX):
            partner = partners[index, slot]
            start = (jnp.maximum(partner, 0) * BLOCK).astype(jnp.int32)
            other = lax.dynamic_slice_in_dim(standard, start, BLOCK, 1)
            tile = lax.dot_general(own, other, (((0,), (0,)), ((), ())), preferred_element_type=jnp.float32) / SAMPLES
            tiles.append(jnp.where(partner >= 0, tile, jnp.zeros_like(tile)))
        return jnp.stack(tiles)
    return lax.map(one_block, jnp.arange(NBLK, dtype=jnp.int32))
```

```python
import functools

import jax
import jax.numpy as jnp
from jax import lax
from jax.experimental import pallas as pl
from jax.experimental.pallas import tpu as pltpu
from jax.sharding import PartitionSpec as P

BLOCK = 512
REACH = 2
HALF = BLOCK // 2
CHUNK = 256
MESH = pl.DeviceIdType.MESH
F32 = jnp.float32
BF16 = jnp.bfloat16
PIECES = ((0, 256), (256, 256), (512, 256), (768, 256))


def tiles_of(start):
    block = 3 + start // BLOCK
    return [(local, block - local) for local in range(3) if block - local <= REACH]


def ld_kernel(
    runs, samples_total, x_hbm, out_ref, xv, sv, svt, halo, hs, part, got, sums, sums_peer,
    stats, halo_stats, load_sem, sum_sems, stat_sems, halo_send, halo_recv, tile_send, tile_recv,
):
    r = lax.axis_index("region")
    s = lax.axis_index("snp")
    c = lax.axis_index("sample")
    peer = (r, s, 1 - c)
    left = (r, s - 1, c)
    right = (r, s + 1, c)
    rows, width = xv.shape
    has_left = s > 0
    has_right = s < runs - 1

    barrier = pltpu.get_barrier_semaphore()
    load = pltpu.make_async_copy(x_hbm, xv, load_sem)
    load.start()
    pl.semaphore_signal(barrier, inc=1, device_id=peer, device_id_type=MESH)

    @pl.when(has_right)
    def _():
        pl.semaphore_signal(barrier, inc=1, device_id=right, device_id_type=MESH)

    pl.semaphore_wait(barrier, jnp.where(has_left, 2, 1))

    def halo_copy(k):
        start, size = PIECES[k]
        cols = pl.ds(start, size)
        return pltpu.make_async_remote_copy(
            x_hbm.at[:, cols], halo.at[:, cols], halo_send.at[k], halo_recv.at[k],
            device_id=left, device_id_type=MESH,
        )

    @pl.when(has_left)
    def _():
        for k in range(2):
            halo_copy(k).start()

    load.wait()

    def add_rows(i, carry):
        a, b = carry
        v = xv[pl.ds(pl.multiple_of(i * 16, 16), 16), :].astype(F32)
        q = v * v
        return a + (v[:8] + v[8:]), b + (q[:8] + q[8:])

    zero = jnp.zeros((8, width), F32)
    a, b = lax.fori_loop(0, rows // 16, add_rows, (zero, zero))
    sums[0:1, :] = jnp.sum(a, axis=0, keepdims=True)
    sums[1:2, :] = jnp.sum(b, axis=0, keepdims=True)
    sums[2:8, :] = jnp.zeros((6, width), F32)
    swap = pltpu.make_async_remote_copy(
        sums, sums_peer, sum_sems.at[0], sum_sems.at[1], device_id=peer, device_id_type=MESH
    )
    swap.start()
    swap.wait()
    both = sums[...] + sums_peer[...]
    mean = both[0:1] / samples_total
    variance = both[1:2] / samples_total - mean * mean
    scale = lax.rsqrt(variance + 1e-05)
    stats[0:1, :] = mean
    stats[1:2, :] = scale
    stats[2:8, :] = jnp.zeros((6, width), F32)
    stat_copy = pltpu.make_async_remote_copy(
        stats.at[:, pl.ds(0, REACH * BLOCK)], halo_stats, stat_sems.at[0], stat_sems.at[1],
        device_id=left, device_id_type=MESH,
    )

    @pl.when(has_left)
    def _():
        stat_copy.start()

    def standardize(i, _):
        at = pl.ds(pl.multiple_of(i * 256, 256), 256)
        for col in range(0, width, BLOCK):
            cols = pl.ds(col, BLOCK)
            v = xv[at, cols].astype(F32)
            w = ((v - stats[0:1, cols]) * stats[1:2, cols]).astype(BF16)
            sv[at, cols] = w
            svt[cols, at] = w.T
        return 0

    lax.fori_loop(0, rows // 256, standardize, 0)

    def tile_copy(n, tile, cols):
        at = pl.ds(pl.multiple_of(tile * BLOCK + (1 - c) * HALF, HALF), HALF)
        return pltpu.make_async_remote_copy(
            part.at[at, cols], got.at[pl.ds(tile * HALF, HALF), cols],
            tile_send.at[n], tile_recv.at[n], device_id=peer, device_id_type=MESH,
        )

    def finish(n, tile, cols):
        copy = tile_copy(n, tile, cols)
        copy.wait()
        own = pl.ds(pl.multiple_of(tile * BLOCK + c * HALF, HALF), HALF)
        at = pl.ds(tile * HALF, HALF)
        out_ref[at, cols] = (part[own, cols] + got[at, cols]) * (1.0 / samples_total)

    whole = pl.ds(0, BLOCK)
    local = [(b0, off) for b0 in range(3) for off in range(3 - b0)]
    for n, (b0, off) in enumerate(local):
        tile = b0 * 3 + off
        part[tile * BLOCK : (tile + 1) * BLOCK, :] = jnp.dot(
            svt[b0 * BLOCK : (b0 + 1) * BLOCK, :],
            sv[:, (b0 + off) * BLOCK : (b0 + off + 1) * BLOCK],
            preferred_element_type=F32,
        )
        tile_copy(n, tile, whole).start()
    for n, (b0, off) in enumerate(local):
        finish(n, b0 * 3 + off, whole)

    @pl.when(has_left)
    def _():
        stat_copy.wait_send()

    @pl.when(has_right)
    def _():
        stat_copy.wait_recv()

    n = len(local)
    pending = []
    for k, (start, size) in enumerate(PIECES):

        @pl.when(has_left)
        def _():
            halo_copy(k).wait_send()
            if k + 2 < len(PIECES):
                halo_copy(k + 2).start()

        here = tiles_of(start)
        at_col = start % BLOCK
        cols = pl.ds(at_col, size)

        @pl.when(has_right)
        def _():
            halo_copy(k).wait_recv()

            def standardize_halo(i, _):
                at = pl.ds(pl.multiple_of(i * 256, 256), 256)
                hc = pl.ds(start, size)
                v = halo[at, hc].astype(F32)
                hs[at, 0:size] = ((v - halo_stats[0:1, hc]) * halo_stats[1:2, hc]).astype(BF16)
                return 0

            lax.fori_loop(0, rows // 256, standardize_halo, 0)
            for j, (b0, off) in enumerate(here):
                tile = b0 * 3 + off
                part[tile * BLOCK : (tile + 1) * BLOCK, at_col : at_col + size] = jnp.dot(
                    svt[b0 * BLOCK : (b0 + 1) * BLOCK, :], hs[:, 0:size],
                    preferred_element_type=F32,
                )
                tile_copy(n + j, tile, cols).start()
            for j, (b0, off) in enumerate(here):
                finish(n + j, b0 * 3 + off, cols)

        n += len(here)

    @pl.when(jnp.logical_not(has_right))
    def _():
        for tile in (5, 7, 8):
            out_ref[tile * HALF : (tile + 1) * HALF, :] = jnp.zeros((HALF, BLOCK), F32)


def pick_kernel(partners_ref, tiles_ref, out_ref):
    b = pl.program_id(0)
    base = partners_ref[b, 0]
    out_ref[0, 0] = tiles_ref[0, 0]
    p1 = partners_ref[b, 1]
    p2 = partners_ref[b, 2]
    one = tiles_ref[0, 1]
    two = tiles_ref[0, 2]
    zero = jnp.zeros_like(one)
    out_ref[0, 1] = jnp.where(p1 < 0, zero, jnp.where(p1 == base + 1, one, two))
    out_ref[0, 2] = jnp.where(p2 < 0, zero, two)


def on_device(dosage, partners):
    rows, width = dosage.shape
    samples_total = rows * lax.axis_size("sample")
    blocks = partners.shape[0]
    tiles = blocks * 3
    n_cross = sum(len(tiles_of(start)) for start, _ in PIECES)
    n_copies = 6 + n_cross
    dma = pltpu.SemaphoreType.DMA
    sums = pl.pallas_call(
        functools.partial(ld_kernel, lax.axis_size("snp"), samples_total),
        out_shape=jax.ShapeDtypeStruct((tiles * HALF, BLOCK), F32),
        in_specs=[pl.BlockSpec(memory_space=pl.ANY)],
        out_specs=pl.BlockSpec(memory_space=pltpu.VMEM),
        scratch_shapes=[
            pltpu.VMEM((rows, width), BF16),
            pltpu.VMEM((rows, width), BF16),
            pltpu.VMEM((width, rows), BF16),
            pltpu.VMEM((rows, REACH * BLOCK), BF16),
            pltpu.VMEM((rows, CHUNK), BF16),
            pltpu.VMEM((tiles * BLOCK, BLOCK), F32),
            pltpu.VMEM((tiles * HALF, BLOCK), F32),
            pltpu.VMEM((8, width), F32),
            pltpu.VMEM((8, width), F32),
            pltpu.VMEM((8, width), F32),
            pltpu.VMEM((8, REACH * BLOCK), F32),
            dma,
            dma((2,)),
            dma((2,)),
            dma((len(PIECES),)),
            dma((len(PIECES),)),
            dma((n_copies,)),
            dma((n_copies,)),
        ],
        compiler_params=pltpu.CompilerParams(
            collective_id=0, has_side_effects=True, vmem_limit_bytes=52 * 2**20
        ),
    )(dosage)
    return pl.pallas_call(
        pick_kernel,
        grid=(blocks,),
        out_shape=jax.ShapeDtypeStruct((blocks, 3, HALF, BLOCK), F32),
        in_specs=[
            pl.BlockSpec(memory_space=pltpu.SMEM),
            pl.BlockSpec((1, 3, HALF, BLOCK), lambda b: (b, 0, 0, 0)),
        ],
        out_specs=pl.BlockSpec((1, 3, HALF, BLOCK), lambda b: (b, 0, 0, 0)),
        compiler_params=pltpu.CompilerParams(vmem_limit_bytes=24 * 2**20),
    )(partners, sums.reshape(blocks, 3, HALF, BLOCK))


def solution(mesh):
    in_specs = (P("sample", ("region", "snp")), P(("region", "snp"), None))
    out_specs = P(("region", "snp"), None, "sample", None)
    return jax.shard_map(
        on_device, mesh=mesh, in_specs=in_specs, out_specs=out_specs, check_vma=False
    )
```

```python
import functools

import jax
import jax.numpy as jnp
from jax import lax
from jax.experimental import pallas as pl
from jax.experimental.pallas import tpu as pltpu
from jax.sharding import PartitionSpec as P

BLOCK = 512
REACH = 2
HALF = BLOCK // 2
CHUNK = 256
MESH = pl.DeviceIdType.MESH
F32 = jnp.float32
BF16 = jnp.bfloat16
PIECES = ((0, 256), (256, 256), (512, 256), (768, 128), (896, 128))


def tiles_of(start):
    block = 3 + start // BLOCK
    return [(local, block - local) for local in range(3) if block - local <= REACH]


def ld_kernel(
    runs, samples_total, x_hbm, out_ref, xv, sv, svt, halo, hs, part, got, sums, sums_peer,
    stats, halo_stats, load_sem, sum_sems, stat_sems, halo_send, halo_recv, tile_send, tile_recv,
):
    r = lax.axis_index("region")
    s = lax.axis_index("snp")
    c = lax.axis_index("sample")
    peer = (r, s, 1 - c)
    left = (r, s - 1, c)
    right = (r, s + 1, c)
    rows, width = xv.shape
    has_left = s > 0
    has_right = s < runs - 1

    barrier = pltpu.get_barrier_semaphore()
    load = pltpu.make_async_copy(x_hbm, xv, load_sem)
    load.start()
    pl.semaphore_signal(barrier, inc=1, device_id=peer, device_id_type=MESH)

    @pl.when(has_right)
    def _():
        pl.semaphore_signal(barrier, inc=1, device_id=right, device_id_type=MESH)

    pl.semaphore_wait(barrier, jnp.where(has_left, 2, 1))

    def halo_copy(k):
        start, size = PIECES[k]
        cols = pl.ds(start, size)
        return pltpu.make_async_remote_copy(
            x_hbm.at[:, cols], halo.at[:, cols], halo_send.at[k], halo_recv.at[k],
            device_id=left, device_id_type=MESH,
        )

    @pl.when(has_left)
    def _():
        for k in range(2):
            halo_copy(k).start()

    load.wait()

    def add_rows(i, carry):
        a, b = carry
        v = xv[pl.ds(pl.multiple_of(i * 16, 16), 16), :].astype(F32)
        q = v * v
        return a + (v[:8] + v[8:]), b + (q[:8] + q[8:])

    zero = jnp.zeros((8, width), F32)
    a, b = lax.fori_loop(0, rows // 16, add_rows, (zero, zero))
    sums[0:1, :] = jnp.sum(a, axis=0, keepdims=True)
    sums[1:2, :] = jnp.sum(b, axis=0, keepdims=True)
    sums[2:8, :] = jnp.zeros((6, width), F32)
    swap = pltpu.make_async_remote_copy(
        sums, sums_peer, sum_sems.at[0], sum_sems.at[1], device_id=peer, device_id_type=MESH
    )
    swap.start()
    swap.wait()
    both = sums[...] + sums_peer[...]
    mean = both[0:1] / samples_total
    variance = both[1:2] / samples_total - mean * mean
    scale = lax.rsqrt(variance + 1e-05)
    stats[0:1, :] = mean
    stats[1:2, :] = scale
    stats[2:8, :] = jnp.zeros((6, width), F32)
    stat_copy = pltpu.make_async_remote_copy(
        stats.at[:, pl.ds(0, REACH * BLOCK)], halo_stats, stat_sems.at[0], stat_sems.at[1],
        device_id=left, device_id_type=MESH,
    )

    @pl.when(has_left)
    def _():
        stat_copy.start()

    def standardize(i, _):
        at = pl.ds(pl.multiple_of(i * 256, 256), 256)
        for col in range(0, width, BLOCK):
            cols = pl.ds(col, BLOCK)
            v = xv[at, cols].astype(F32)
            w = ((v - stats[0:1, cols]) * stats[1:2, cols]).astype(BF16)
            sv[at, cols] = w
            svt[cols, at] = w.T
        return 0

    lax.fori_loop(0, rows // 256, standardize, 0)

    def tile_copy(n, tile, cols):
        at = pl.ds(pl.multiple_of(tile * BLOCK + (1 - c) * HALF, HALF), HALF)
        return pltpu.make_async_remote_copy(
            part.at[at, cols], got.at[pl.ds(tile * HALF, HALF), cols],
            tile_send.at[n], tile_recv.at[n], device_id=peer, device_id_type=MESH,
        )

    def finish(n, tile, cols):
        copy = tile_copy(n, tile, cols)
        copy.wait()
        own = pl.ds(pl.multiple_of(tile * BLOCK + c * HALF, HALF), HALF)
        at = pl.ds(tile * HALF, HALF)
        out_ref[at, cols] = (part[own, cols] + got[at, cols]) * (1.0 / samples_total)

    whole = pl.ds(0, BLOCK)
    local = [(b0, off) for b0 in range(3) for off in range(3 - b0)]
    for n, (b0, off) in enumerate(local):
        tile = b0 * 3 + off
        part[tile * BLOCK : (tile + 1) * BLOCK, :] = jnp.dot(
            svt[b0 * BLOCK : (b0 + 1) * BLOCK, :],
            sv[:, (b0 + off) * BLOCK : (b0 + off + 1) * BLOCK],
            preferred_element_type=F32,
        )
        tile_copy(n, tile, whole).start()
    for n, (b0, off) in enumerate(local):
        finish(n, b0 * 3 + off, whole)

    @pl.when(has_left)
    def _():
        stat_copy.wait_send()

    @pl.when(has_right)
    def _():
        stat_copy.wait_recv()

    n = len(local)
    pending = []
    for k, (start, size) in enumerate(PIECES):

        @pl.when(has_left)
        def _():
            halo_copy(k).wait_send()
            if k + 2 < len(PIECES):
                halo_copy(k + 2).start()

        here = tiles_of(start)
        at_col = start % BLOCK
        cols = pl.ds(at_col, size)

        @pl.when(has_right)
        def _():
            halo_copy(k).wait_recv()

            def standardize_halo(i, _):
                at = pl.ds(pl.multiple_of(i * 256, 256), 256)
                hc = pl.ds(start, size)
                v = halo[at, hc].astype(F32)
                hs[at, 0:size] = ((v - halo_stats[0:1, hc]) * halo_stats[1:2, hc]).astype(BF16)
                return 0

            lax.fori_loop(0, rows // 256, standardize_halo, 0)
            for half in (1 - c, c):
                for j, (b0, off) in enumerate(here):
                    tile = b0 * 3 + off
                    mine = pl.ds(pl.multiple_of(b0 * BLOCK + half * HALF, HALF), HALF)
                    at = pl.ds(pl.multiple_of(tile * BLOCK + half * HALF, HALF), HALF)
                    part[at, cols] = jnp.dot(
                        svt[mine, :], hs[:, 0:size], preferred_element_type=F32
                    )
                    if half is not c:
                        tile_copy(n + j, tile, cols).start()
            for j, (b0, off) in enumerate(here):
                finish(n + j, b0 * 3 + off, cols)

        n += len(here)

    @pl.when(jnp.logical_not(has_right))
    def _():
        for tile in (5, 7, 8):
            out_ref[tile * HALF : (tile + 1) * HALF, :] = jnp.zeros((HALF, BLOCK), F32)


def pick_kernel(partners_ref, tiles_ref, out_ref, zeros, sems):
    blocks = out_ref.shape[0]
    zeros[...] = jnp.zeros_like(zeros)

    def copy(b, slot, src):
        return pltpu.make_async_copy(src, out_ref.at[b, slot], sems.at[b * 3 + slot])

    def tile(b, off):
        return tiles_ref.at[pl.ds((b * 3 + off) * HALF, HALF)]

    for b in range(blocks):
        base = partners_ref[b, 0]
        p1 = partners_ref[b, 1]
        p2 = partners_ref[b, 2]
        copy(b, 0, tile(b, 0)).start()

        @pl.when(p1 == base + 1)
        def _():
            copy(b, 1, tile(b, 1)).start()

        @pl.when(p1 == base + 2)
        def _():
            copy(b, 1, tile(b, 2)).start()

        @pl.when(p1 < 0)
        def _():
            copy(b, 1, zeros).start()

        @pl.when(p2 >= 0)
        def _():
            copy(b, 2, tile(b, 2)).start()

        @pl.when(p2 < 0)
        def _():
            copy(b, 2, zeros).start()

    for b in range(blocks):
        for slot in range(3):
            copy(b, slot, zeros).wait()


def on_device(dosage, partners):
    rows, width = dosage.shape
    samples_total = rows * lax.axis_size("sample")
    blocks = partners.shape[0]
    tiles = blocks * 3
    n_cross = sum(len(tiles_of(start)) for start, _ in PIECES)
    n_copies = 6 + n_cross
    dma = pltpu.SemaphoreType.DMA
    sums = pl.pallas_call(
        functools.partial(ld_kernel, lax.axis_size("snp"), samples_total),
        out_shape=pltpu.VMEM((tiles * HALF, BLOCK), F32),
        in_specs=[pl.BlockSpec(memory_space=pl.ANY)],
        out_specs=pl.BlockSpec(memory_space=pltpu.VMEM),
        scratch_shapes=[
            pltpu.VMEM((rows, width), BF16),
            pltpu.VMEM((rows, width), BF16),
            pltpu.VMEM((width, rows), BF16),
            pltpu.VMEM((rows, REACH * BLOCK), BF16),
            pltpu.VMEM((rows, CHUNK), BF16),
            pltpu.VMEM((tiles * BLOCK, BLOCK), F32),
            pltpu.VMEM((tiles * HALF, BLOCK), F32),
            pltpu.VMEM((8, width), F32),
            pltpu.VMEM((8, width), F32),
            pltpu.VMEM((8, width), F32),
            pltpu.VMEM((8, REACH * BLOCK), F32),
            dma,
            dma((2,)),
            dma((2,)),
            dma((len(PIECES),)),
            dma((len(PIECES),)),
            dma((n_copies,)),
            dma((n_copies,)),
        ],
        compiler_params=pltpu.CompilerParams(
            collective_id=0, has_side_effects=True, vmem_limit_bytes=52 * 2**20
        ),
    )(dosage)
    return pl.pallas_call(
        pick_kernel,
        out_shape=jax.ShapeDtypeStruct((blocks, 3, HALF, BLOCK), F32),
        in_specs=[
            pl.BlockSpec(memory_space=pltpu.SMEM),
            pl.BlockSpec(memory_space=pltpu.VMEM),
        ],
        out_specs=pl.BlockSpec(memory_space=pl.ANY),
        scratch_shapes=[pltpu.VMEM((HALF, BLOCK), F32), dma((tiles,))],
        compiler_params=pltpu.CompilerParams(vmem_limit_bytes=16 * 2**20),
    )(partners, sums)


def solution(mesh):
    in_specs = (P("sample", ("region", "snp")), P(("region", "snp"), None))
    out_specs = P(("region", "snp"), None, "sample", None)
    return jax.shard_map(
        on_device, mesh=mesh, in_specs=in_specs, out_specs=out_specs, check_vma=False
    )
```

```python
import functools

import jax
import jax.numpy as jnp
from jax import lax
from jax.experimental import pallas as pl
from jax.experimental.pallas import tpu as pltpu
from jax.sharding import PartitionSpec as P

BLOCK = 512
REACH = 2
HALF = BLOCK // 2
CHUNK = 256
MESH = pl.DeviceIdType.MESH
F32 = jnp.float32
BF16 = jnp.bfloat16
AHEAD = 3
PIECES = ((0, 256), (256, 256), (512, 256), (768, 128), (896, 128))


def tiles_of(start):
    block = 3 + start // BLOCK
    return [(local, block - local) for local in range(3) if block - local <= REACH]


def ld_kernel(
    runs, samples_total, x_hbm, out_ref, xv, sv, svt, halo, hs, part, got, sums, sums_peer,
    stats, halo_stats, load_sem, sum_sems, stat_sems, halo_send, halo_recv, tile_send, tile_recv,
):
    r = lax.axis_index("region")
    s = lax.axis_index("snp")
    c = lax.axis_index("sample")
    peer = (r, s, 1 - c)
    left = (r, s - 1, c)
    right = (r, s + 1, c)
    rows, width = xv.shape
    has_left = s > 0
    has_right = s < runs - 1

    barrier = pltpu.get_barrier_semaphore()
    load = pltpu.make_async_copy(x_hbm, xv, load_sem)
    load.start()
    pl.semaphore_signal(barrier, inc=1, device_id=peer, device_id_type=MESH)

    @pl.when(has_right)
    def _():
        pl.semaphore_signal(barrier, inc=1, device_id=right, device_id_type=MESH)

    pl.semaphore_wait(barrier, jnp.where(has_left, 2, 1))

    def halo_copy(k):
        start, size = PIECES[k]
        cols = pl.ds(start, size)
        return pltpu.make_async_remote_copy(
            x_hbm.at[:, cols], halo.at[:, cols], halo_send.at[k], halo_recv.at[k],
            device_id=left, device_id_type=MESH,
        )

    @pl.when(has_left)
    def _():
        for k in range(AHEAD):
            halo_copy(k).start()

    load.wait()

    def add_rows(i, carry):
        a, b = carry
        v = xv[pl.ds(pl.multiple_of(i * 16, 16), 16), :].astype(F32)
        q = v * v
        return a + (v[:8] + v[8:]), b + (q[:8] + q[8:])

    zero = jnp.zeros((8, width), F32)
    a, b = lax.fori_loop(0, rows // 16, add_rows, (zero, zero))
    sums[0:1, :] = jnp.sum(a, axis=0, keepdims=True)
    sums[1:2, :] = jnp.sum(b, axis=0, keepdims=True)
    sums[2:8, :] = jnp.zeros((6, width), F32)
    swap = pltpu.make_async_remote_copy(
        sums, sums_peer, sum_sems.at[0], sum_sems.at[1], device_id=peer, device_id_type=MESH
    )
    swap.start()
    swap.wait()
    both = sums[...] + sums_peer[...]
    mean = both[0:1] / samples_total
    variance = both[1:2] / samples_total - mean * mean
    scale = lax.rsqrt(variance + 1e-05)
    stats[0:1, :] = mean
    stats[1:2, :] = scale
    stats[2:8, :] = jnp.zeros((6, width), F32)
    stat_copy = pltpu.make_async_remote_copy(
        stats.at[:, pl.ds(0, REACH * BLOCK)], halo_stats, stat_sems.at[0], stat_sems.at[1],
        device_id=left, device_id_type=MESH,
    )

    @pl.when(has_left)
    def _():
        stat_copy.start()

    def standardize(i, _):
        at = pl.ds(pl.multiple_of(i * 256, 256), 256)
        for col in range(0, width, BLOCK):
            cols = pl.ds(col, BLOCK)
            v = xv[at, cols].astype(F32)
            w = ((v - stats[0:1, cols]) * stats[1:2, cols]).astype(BF16)
            sv[at, cols] = w
            svt[cols, at] = w.T
        return 0

    lax.fori_loop(0, rows // 256, standardize, 0)

    def tile_copy(n, tile, cols):
        at = pl.ds(pl.multiple_of(tile * BLOCK + (1 - c) * HALF, HALF), HALF)
        return pltpu.make_async_remote_copy(
            part.at[at, cols], got.at[pl.ds(tile * HALF, HALF), cols],
            tile_send.at[n], tile_recv.at[n], device_id=peer, device_id_type=MESH,
        )

    def finish(n, tile, cols):
        copy = tile_copy(n, tile, cols)
        copy.wait()
        own = pl.ds(pl.multiple_of(tile * BLOCK + c * HALF, HALF), HALF)
        at = pl.ds(tile * HALF, HALF)
        out_ref[at, cols] = (part[own, cols] + got[at, cols]) * (1.0 / samples_total)

    whole = pl.ds(0, BLOCK)
    local = [(b0, off) for b0 in range(3) for off in range(3 - b0)]
    for n, (b0, off) in enumerate(local):
        tile = b0 * 3 + off
        part[tile * BLOCK : (tile + 1) * BLOCK, :] = jnp.dot(
            svt[b0 * BLOCK : (b0 + 1) * BLOCK, :],
            sv[:, (b0 + off) * BLOCK : (b0 + off + 1) * BLOCK],
            preferred_element_type=F32,
        )
        tile_copy(n, tile, whole).start()
    for n, (b0, off) in enumerate(local):
        finish(n, b0 * 3 + off, whole)

    @pl.when(has_left)
    def _():
        stat_copy.wait_send()

    @pl.when(has_right)
    def _():
        stat_copy.wait_recv()

    n = len(local)
    pending = []
    for k, (start, size) in enumerate(PIECES):

        @pl.when(has_left)
        def _():
            halo_copy(k).wait_send()
            if k + AHEAD < len(PIECES):
                halo_copy(k + AHEAD).start()

        here = tiles_of(start)
        at_col = start % BLOCK
        cols = pl.ds(at_col, size)

        @pl.when(has_right)
        def _():
            halo_copy(k).wait_recv()

            def standardize_halo(i, _):
                at = pl.ds(pl.multiple_of(i * 256, 256), 256)
                hc = pl.ds(start, size)
                v = halo[at, hc].astype(F32)
                hs[at, 0:size] = ((v - halo_stats[0:1, hc]) * halo_stats[1:2, hc]).astype(BF16)
                return 0

            lax.fori_loop(0, rows // 256, standardize_halo, 0)
            for half in (1 - c, c):
                for j, (b0, off) in enumerate(here):
                    tile = b0 * 3 + off
                    mine = pl.ds(pl.multiple_of(b0 * BLOCK + half * HALF, HALF), HALF)
                    at = pl.ds(pl.multiple_of(tile * BLOCK + half * HALF, HALF), HALF)
                    part[at, cols] = jnp.dot(
                        svt[mine, :], hs[:, 0:size], preferred_element_type=F32
                    )
                    if half is not c:
                        tile_copy(n + j, tile, cols).start()
            for j, (b0, off) in enumerate(here):
                finish(n + j, b0 * 3 + off, cols)

        n += len(here)

    @pl.when(jnp.logical_not(has_right))
    def _():
        for tile in (5, 7, 8):
            out_ref[tile * HALF : (tile + 1) * HALF, :] = jnp.zeros((HALF, BLOCK), F32)


def pick_kernel(partners_ref, tiles_ref, out_ref, zeros, sems):
    blocks = out_ref.shape[0]
    zeros[...] = jnp.zeros_like(zeros)

    def copy(b, slot, src):
        return pltpu.make_async_copy(src, out_ref.at[b, slot], sems.at[b * 3 + slot])

    def tile(b, off):
        return tiles_ref.at[pl.ds((b * 3 + off) * HALF, HALF)]

    for b in range(blocks):
        base = partners_ref[b, 0]
        p1 = partners_ref[b, 1]
        p2 = partners_ref[b, 2]
        copy(b, 0, tile(b, 0)).start()

        @pl.when(p1 == base + 1)
        def _():
            copy(b, 1, tile(b, 1)).start()

        @pl.when(p1 == base + 2)
        def _():
            copy(b, 1, tile(b, 2)).start()

        @pl.when(p1 < 0)
        def _():
            copy(b, 1, zeros).start()

        @pl.when(p2 >= 0)
        def _():
            copy(b, 2, tile(b, 2)).start()

        @pl.when(p2 < 0)
        def _():
            copy(b, 2, zeros).start()

    for b in range(blocks):
        for slot in range(3):
            copy(b, slot, zeros).wait()


def on_device(dosage, partners):
    rows, width = dosage.shape
    samples_total = rows * lax.axis_size("sample")
    blocks = partners.shape[0]
    tiles = blocks * 3
    n_cross = sum(len(tiles_of(start)) for start, _ in PIECES)
    n_copies = 6 + n_cross
    dma = pltpu.SemaphoreType.DMA
    sums = pl.pallas_call(
        functools.partial(ld_kernel, lax.axis_size("snp"), samples_total),
        out_shape=pltpu.VMEM((tiles * HALF, BLOCK), F32),
        in_specs=[pl.BlockSpec(memory_space=pl.ANY)],
        out_specs=pl.BlockSpec(memory_space=pltpu.VMEM),
        scratch_shapes=[
            pltpu.VMEM((rows, width), BF16),
            pltpu.VMEM((rows, width), BF16),
            pltpu.VMEM((width, rows), BF16),
            pltpu.VMEM((rows, REACH * BLOCK), BF16),
            pltpu.VMEM((rows, CHUNK), BF16),
            pltpu.VMEM((tiles * BLOCK, BLOCK), F32),
            pltpu.VMEM((tiles * HALF, BLOCK), F32),
            pltpu.VMEM((8, width), F32),
            pltpu.VMEM((8, width), F32),
            pltpu.VMEM((8, width), F32),
            pltpu.VMEM((8, REACH * BLOCK), F32),
            dma,
            dma((2,)),
            dma((2,)),
            dma((len(PIECES),)),
            dma((len(PIECES),)),
            dma((n_copies,)),
            dma((n_copies,)),
        ],
        compiler_params=pltpu.CompilerParams(
            collective_id=0, has_side_effects=True, vmem_limit_bytes=52 * 2**20
        ),
    )(dosage)
    return pl.pallas_call(
        pick_kernel,
        out_shape=jax.ShapeDtypeStruct((blocks, 3, HALF, BLOCK), F32),
        in_specs=[
            pl.BlockSpec(memory_space=pltpu.SMEM),
            pl.BlockSpec(memory_space=pltpu.VMEM),
        ],
        out_specs=pl.BlockSpec(memory_space=pl.ANY),
        scratch_shapes=[pltpu.VMEM((HALF, BLOCK), F32), dma((tiles,))],
        compiler_params=pltpu.CompilerParams(vmem_limit_bytes=16 * 2**20),
    )(partners, sums)


def solution(mesh):
    in_specs = (P("sample", ("region", "snp")), P(("region", "snp"), None))
    out_specs = P(("region", "snp"), None, "sample", None)
    return jax.shard_map(
        on_device, mesh=mesh, in_specs=in_specs, out_specs=out_specs, check_vma=False
    )
```

```python
import functools

import jax
import jax.numpy as jnp
from jax import lax
from jax.experimental import pallas as pl
from jax.experimental.pallas import tpu as pltpu
from jax.sharding import PartitionSpec as P

BLOCK = 512
REACH = 2
HALF = BLOCK // 2
CHUNK = 256
MESH = pl.DeviceIdType.MESH
F32 = jnp.float32
BF16 = jnp.bfloat16
PIECES = (
    (0, 256, 0, 8),
    (256, 256, 0, 8),
    (512, 256, 0, 8),
    (768, 128, 0, 8),
    (896, 128, 0, 6),
    (896, 128, 6, 8),
)


def tiles_of(start):
    block = 3 + start // BLOCK
    return [(local, block - local) for local in range(3) if block - local <= REACH]


def ld_kernel(
    runs, samples_total, x_hbm, out_ref, xv, sv, svt, halo, hs, part, got, sums, sums_peer,
    stats, halo_stats, load_sem, sum_sems, stat_sems, halo_send, halo_recv, tile_send, tile_recv,
):
    r = lax.axis_index("region")
    s = lax.axis_index("snp")
    c = lax.axis_index("sample")
    peer = (r, s, 1 - c)
    left = (r, s - 1, c)
    right = (r, s + 1, c)
    rows, width = xv.shape
    has_left = s > 0
    has_right = s < runs - 1

    barrier = pltpu.get_barrier_semaphore()
    load = pltpu.make_async_copy(x_hbm, xv, load_sem)
    load.start()
    pl.semaphore_signal(barrier, inc=1, device_id=peer, device_id_type=MESH)

    @pl.when(has_right)
    def _():
        pl.semaphore_signal(barrier, inc=1, device_id=right, device_id_type=MESH)

    pl.semaphore_wait(barrier, jnp.where(has_left, 2, 1))

    def halo_copy(k):
        start, size, first, last = PIECES[k]
        cols = pl.ds(start, size)
        at = pl.ds(first * rows // 8, (last - first) * rows // 8)
        return pltpu.make_async_remote_copy(
            x_hbm.at[at, cols], halo.at[at, cols], halo_send.at[k], halo_recv.at[k],
            device_id=left, device_id_type=MESH,
        )

    @pl.when(has_left)
    def _():
        for k in range(2):
            halo_copy(k).start()

    load.wait()

    def add_rows(i, carry):
        a, b = carry
        v = xv[pl.ds(pl.multiple_of(i * 16, 16), 16), :].astype(F32)
        q = v * v
        return a + (v[:8] + v[8:]), b + (q[:8] + q[8:])

    zero = jnp.zeros((8, width), F32)
    a, b = lax.fori_loop(0, rows // 16, add_rows, (zero, zero))
    sums[0:1, :] = jnp.sum(a, axis=0, keepdims=True)
    sums[1:2, :] = jnp.sum(b, axis=0, keepdims=True)
    sums[2:8, :] = jnp.zeros((6, width), F32)
    swap = pltpu.make_async_remote_copy(
        sums, sums_peer, sum_sems.at[0], sum_sems.at[1], device_id=peer, device_id_type=MESH
    )
    swap.start()
    swap.wait()
    both = sums[...] + sums_peer[...]
    mean = both[0:1] / samples_total
    variance = both[1:2] / samples_total - mean * mean
    scale = lax.rsqrt(variance + 1e-05)
    stats[0:1, :] = mean
    stats[1:2, :] = scale
    stats[2:8, :] = jnp.zeros((6, width), F32)
    stat_copy = pltpu.make_async_remote_copy(
        stats.at[:, pl.ds(0, REACH * BLOCK)], halo_stats, stat_sems.at[0], stat_sems.at[1],
        device_id=left, device_id_type=MESH,
    )

    @pl.when(has_left)
    def _():
        stat_copy.start()

    def standardize(i, _):
        at = pl.ds(pl.multiple_of(i * 256, 256), 256)
        for col in range(0, width, BLOCK):
            cols = pl.ds(col, BLOCK)
            v = xv[at, cols].astype(F32)
            w = ((v - stats[0:1, cols]) * stats[1:2, cols]).astype(BF16)
            sv[at, cols] = w
            svt[cols, at] = w.T
        return 0

    lax.fori_loop(0, rows // 256, standardize, 0)

    def tile_copy(n, tile, cols):
        at = pl.ds(pl.multiple_of(tile * BLOCK + (1 - c) * HALF, HALF), HALF)
        return pltpu.make_async_remote_copy(
            part.at[at, cols], got.at[pl.ds(tile * HALF, HALF), cols],
            tile_send.at[n], tile_recv.at[n], device_id=peer, device_id_type=MESH,
        )

    def finish(n, tile, cols):
        copy = tile_copy(n, tile, cols)
        copy.wait()
        own = pl.ds(pl.multiple_of(tile * BLOCK + c * HALF, HALF), HALF)
        at = pl.ds(tile * HALF, HALF)
        out_ref[at, cols] = (part[own, cols] + got[at, cols]) * (1.0 / samples_total)

    whole = pl.ds(0, BLOCK)
    local = [(b0, off) for b0 in range(3) for off in range(3 - b0)]
    for n, (b0, off) in enumerate(local):
        tile = b0 * 3 + off
        part[tile * BLOCK : (tile + 1) * BLOCK, :] = jnp.dot(
            svt[b0 * BLOCK : (b0 + 1) * BLOCK, :],
            sv[:, (b0 + off) * BLOCK : (b0 + off + 1) * BLOCK],
            preferred_element_type=F32,
        )
        tile_copy(n, tile, whole).start()
    for n, (b0, off) in enumerate(local):
        finish(n, b0 * 3 + off, whole)

    @pl.when(has_left)
    def _():
        stat_copy.wait_send()

    @pl.when(has_right)
    def _():
        stat_copy.wait_recv()

    n = len(local)
    pending = []
    for k, (start, size, first, last) in enumerate(PIECES):

        @pl.when(has_left)
        def _():
            halo_copy(k).wait_send()
            if k + 2 < len(PIECES):
                halo_copy(k + 2).start()

        here = tiles_of(start)
        at_col = start % BLOCK
        cols = pl.ds(at_col, size)

        @pl.when(has_right)
        def _():
            halo_copy(k).wait_recv()

            def standardize_halo(i, _):
                at = pl.ds(pl.multiple_of(i * 256, 256), 256)
                hc = pl.ds(start, size)
                v = halo[at, hc].astype(F32)
                hs[at, 0:size] = ((v - halo_stats[0:1, hc]) * halo_stats[1:2, hc]).astype(BF16)
                return 0

            row0, row1 = first * rows // 8, last * rows // 8
            lax.fori_loop(row0 // 256, row1 // 256, standardize_halo, 0)
            for half in (1 - c, c):
                for j, (b0, off) in enumerate(here):
                    tile = b0 * 3 + off
                    mine = pl.ds(pl.multiple_of(b0 * BLOCK + half * HALF, HALF), HALF)
                    at = pl.ds(pl.multiple_of(tile * BLOCK + half * HALF, HALF), HALF)
                    term = jnp.dot(
                        svt[mine, row0:row1], hs[row0:row1, 0:size], preferred_element_type=F32
                    )
                    part[at, cols] = term if first == 0 else part[at, cols] + term
                    if half is not c and last == 8:
                        tile_copy(n + j, tile, cols).start()
            if last == 8:
                for j, (b0, off) in enumerate(here):
                    finish(n + j, b0 * 3 + off, cols)

        if last == 8:
            n += len(here)

    @pl.when(jnp.logical_not(has_right))
    def _():
        for tile in (5, 7, 8):
            out_ref[tile * HALF : (tile + 1) * HALF, :] = jnp.zeros((HALF, BLOCK), F32)


def pick_kernel(partners_ref, tiles_ref, out_ref, zeros, sems):
    blocks = out_ref.shape[0]
    def copy(b, slot, src):
        return pltpu.make_async_copy(src, out_ref.at[b, slot], sems.at[b * 3 + slot])

    def tile(b, off):
        return tiles_ref.at[pl.ds((b * 3 + off) * HALF, HALF)]

    for b in range(blocks):
        copy(b, 0, tile(b, 0)).start()
    zeros[...] = jnp.zeros_like(zeros)
    for b in range(blocks):
        base = partners_ref[b, 0]
        p1 = partners_ref[b, 1]
        p2 = partners_ref[b, 2]

        @pl.when(p1 == base + 1)
        def _():
            copy(b, 1, tile(b, 1)).start()

        @pl.when(p1 == base + 2)
        def _():
            copy(b, 1, tile(b, 2)).start()

        @pl.when(p1 < 0)
        def _():
            copy(b, 1, zeros).start()

        @pl.when(p2 >= 0)
        def _():
            copy(b, 2, tile(b, 2)).start()

        @pl.when(p2 < 0)
        def _():
            copy(b, 2, zeros).start()

    for b in range(blocks):
        for slot in range(3):
            copy(b, slot, zeros).wait()


def on_device(dosage, partners):
    rows, width = dosage.shape
    samples_total = rows * lax.axis_size("sample")
    blocks = partners.shape[0]
    tiles = blocks * 3
    n_cross = sum(len(tiles_of(start)) for start, _, _, last in PIECES if last == 8)
    n_copies = 6 + n_cross
    dma = pltpu.SemaphoreType.DMA
    sums = pl.pallas_call(
        functools.partial(ld_kernel, lax.axis_size("snp"), samples_total),
        out_shape=pltpu.VMEM((tiles * HALF, BLOCK), F32),
        in_specs=[pl.BlockSpec(memory_space=pl.ANY)],
        out_specs=pl.BlockSpec(memory_space=pltpu.VMEM),
        scratch_shapes=[
            pltpu.VMEM((rows, width), BF16),
            pltpu.VMEM((rows, width), BF16),
            pltpu.VMEM((width, rows), BF16),
            pltpu.VMEM((rows, REACH * BLOCK), BF16),
            pltpu.VMEM((rows, CHUNK), BF16),
            pltpu.VMEM((tiles * BLOCK, BLOCK), F32),
            pltpu.VMEM((tiles * HALF, BLOCK), F32),
            pltpu.VMEM((8, width), F32),
            pltpu.VMEM((8, width), F32),
            pltpu.VMEM((8, width), F32),
            pltpu.VMEM((8, REACH * BLOCK), F32),
            dma,
            dma((2,)),
            dma((2,)),
            dma((len(PIECES),)),
            dma((len(PIECES),)),
            dma((n_copies,)),
            dma((n_copies,)),
        ],
        compiler_params=pltpu.CompilerParams(
            collective_id=0, has_side_effects=True, vmem_limit_bytes=52 * 2**20
        ),
    )(dosage)
    return pl.pallas_call(
        pick_kernel,
        out_shape=jax.ShapeDtypeStruct((blocks, 3, HALF, BLOCK), F32),
        in_specs=[
            pl.BlockSpec(memory_space=pltpu.SMEM),
            pl.BlockSpec(memory_space=pltpu.VMEM),
        ],
        out_specs=pl.BlockSpec(memory_space=pl.ANY),
        scratch_shapes=[pltpu.VMEM((HALF, BLOCK), F32), dma((tiles,))],
        compiler_params=pltpu.CompilerParams(vmem_limit_bytes=16 * 2**20),
    )(partners, sums)


def solution(mesh):
    in_specs = (P("sample", ("region", "snp")), P(("region", "snp"), None))
    out_specs = P(("region", "snp"), None, "sample", None)
    return jax.shard_map(
        on_device, mesh=mesh, in_specs=in_specs, out_specs=out_specs, check_vma=False
    )
```

```python
import functools

import jax
import jax.numpy as jnp
from jax import lax
from jax.experimental import pallas as pl
from jax.experimental.pallas import tpu as pltpu
from jax.sharding import PartitionSpec as P

BLOCK = 512
REACH = 2
HALF = BLOCK // 2
CHUNK = 256
MESH = pl.DeviceIdType.MESH
F32 = jnp.float32
BF16 = jnp.bfloat16
PIECES = (
    (0, 256, 0, 8),
    (256, 256, 0, 8),
    (512, 256, 0, 8),
    (768, 128, 0, 8),
    (896, 128, 0, 6),
    (896, 128, 6, 8),
)


def tiles_of(start):
    block = 3 + start // BLOCK
    return [(local, block - local) for local in range(3) if block - local <= REACH]


def ld_kernel(
    runs, samples_total, x_hbm, out_ref, xv, sv, svt, halo, hs, part, got, sums, sums_peer,
    stats, halo_stats, load_sem, sum_sems, stat_sems, halo_send, halo_recv, tile_send, tile_recv,
):
    r = lax.axis_index("region")
    s = lax.axis_index("snp")
    c = lax.axis_index("sample")
    peer = (r, s, 1 - c)
    left = (r, s - 1, c)
    right = (r, s + 1, c)
    rows, width = xv.shape
    has_left = s > 0
    has_right = s < runs - 1

    barrier = pltpu.get_barrier_semaphore()
    load = pltpu.make_async_copy(x_hbm, xv, load_sem)
    load.start()
    pl.semaphore_signal(barrier, inc=1, device_id=peer, device_id_type=MESH)

    @pl.when(has_right)
    def _():
        pl.semaphore_signal(barrier, inc=1, device_id=right, device_id_type=MESH)

    pl.semaphore_wait(barrier, jnp.where(has_left, 2, 1))

    def halo_copy(k):
        start, size, first, last = PIECES[k]
        cols = pl.ds(start, size)
        at = pl.ds(first * rows // 8, (last - first) * rows // 8)
        return pltpu.make_async_remote_copy(
            x_hbm.at[at, cols], halo.at[at, cols], halo_send.at[k], halo_recv.at[k],
            device_id=left, device_id_type=MESH,
        )

    @pl.when(has_left)
    def _():
        for k in range(2):
            halo_copy(k).start()

    load.wait()

    def add_rows(i, carry):
        a, b = carry
        v = xv[pl.ds(pl.multiple_of(i * 16, 16), 16), :].astype(F32)
        q = v * v
        return a + (v[:8] + v[8:]), b + (q[:8] + q[8:])

    zero = jnp.zeros((8, width), F32)
    a, b = lax.fori_loop(0, rows // 16, add_rows, (zero, zero))
    sums[0:1, :] = jnp.sum(a, axis=0, keepdims=True)
    sums[1:2, :] = jnp.sum(b, axis=0, keepdims=True)
    sums[2:8, :] = jnp.zeros((6, width), F32)
    swap = pltpu.make_async_remote_copy(
        sums, sums_peer, sum_sems.at[0], sum_sems.at[1], device_id=peer, device_id_type=MESH
    )
    swap.start()
    swap.wait()
    both = sums[...] + sums_peer[...]
    mean = both[0:1] / samples_total
    variance = both[1:2] / samples_total - mean * mean
    scale = lax.rsqrt(variance + 1e-05)
    stats[0:1, :] = mean
    stats[1:2, :] = scale
    stats[2:8, :] = jnp.zeros((6, width), F32)
    stat_copy = pltpu.make_async_remote_copy(
        stats.at[:, pl.ds(0, REACH * BLOCK)], halo_stats, stat_sems.at[0], stat_sems.at[1],
        device_id=left, device_id_type=MESH,
    )

    @pl.when(has_left)
    def _():
        stat_copy.start()

    def standardize(i, _):
        at = pl.ds(pl.multiple_of(i * 256, 256), 256)
        for col in range(0, width, BLOCK):
            cols = pl.ds(col, BLOCK)
            v = xv[at, cols].astype(F32)
            w = ((v - stats[0:1, cols]) * stats[1:2, cols]).astype(BF16)
            sv[at, cols] = w
            svt[cols, at] = w.T
        return 0

    lax.fori_loop(0, rows // 256, standardize, 0)

    def tile_copy(n, tile, cols):
        at = pl.ds(pl.multiple_of(tile * BLOCK + (1 - c) * HALF, HALF), HALF)
        return pltpu.make_async_remote_copy(
            part.at[at, cols], got.at[pl.ds(tile * HALF, HALF), cols],
            tile_send.at[n], tile_recv.at[n], device_id=peer, device_id_type=MESH,
        )

    def finish(n, tile, cols):
        copy = tile_copy(n, tile, cols)
        copy.wait()
        own = pl.ds(pl.multiple_of(tile * BLOCK + c * HALF, HALF), HALF)
        at = pl.ds(tile * HALF, HALF)
        out_ref[at, cols] = (part[own, cols] + got[at, cols]) * (1.0 / samples_total)

    whole = pl.ds(0, BLOCK)
    local = [(b0, off) for b0 in range(3) for off in range(3 - b0)]
    for n, (b0, off) in enumerate(local):
        tile = b0 * 3 + off
        part[tile * BLOCK : (tile + 1) * BLOCK, :] = jnp.dot(
            svt[b0 * BLOCK : (b0 + 1) * BLOCK, :],
            sv[:, (b0 + off) * BLOCK : (b0 + off + 1) * BLOCK],
            preferred_element_type=F32,
        )
        tile_copy(n, tile, whole).start()
    for n, (b0, off) in enumerate(local):
        finish(n, b0 * 3 + off, whole)

    @pl.when(has_left)
    def _():
        stat_copy.wait_send()

    @pl.when(has_right)
    def _():
        stat_copy.wait_recv()

    n = len(local)
    pending = []
    for k, (start, size, first, last) in enumerate(PIECES):

        @pl.when(has_left)
        def _():
            halo_copy(k).wait_send()
            if k + 2 < len(PIECES):
                halo_copy(k + 2).start()

        here = tiles_of(start)
        at_col = start % BLOCK
        cols = pl.ds(at_col, size)

        @pl.when(has_right)
        def _():
            halo_copy(k).wait_recv()

            def standardize_halo(i, _):
                at = pl.ds(pl.multiple_of(i * 256, 256), 256)
                hc = pl.ds(start, size)
                v = halo[at, hc].astype(F32)
                hs[at, 0:size] = ((v - halo_stats[0:1, hc]) * halo_stats[1:2, hc]).astype(BF16)
                return 0

            row0, row1 = first * rows // 8, last * rows // 8
            lax.fori_loop(row0 // 256, row1 // 256, standardize_halo, 0)
            for half in (1 - c, c):
                for j, (b0, off) in enumerate(here):
                    tile = b0 * 3 + off
                    mine = pl.ds(pl.multiple_of(b0 * BLOCK + half * HALF, HALF), HALF)
                    at = pl.ds(pl.multiple_of(tile * BLOCK + half * HALF, HALF), HALF)
                    term = jnp.dot(
                        svt[mine, row0:row1], hs[row0:row1, 0:size], preferred_element_type=F32
                    )
                    part[at, cols] = term if first == 0 else part[at, cols] + term
                    if half is not c and last == 8:
                        tile_copy(n + j, tile, cols).start()
            if last == 8:
                for j, (b0, off) in enumerate(here):
                    finish(n + j, b0 * 3 + off, cols)

        if last == 8:
            n += len(here)

    @pl.when(jnp.logical_not(has_right))
    def _():
        for tile in (5, 7, 8):
            out_ref[tile * HALF : (tile + 1) * HALF, :] = jnp.zeros((HALF, BLOCK), F32)


def pick_kernel(partners_any, tiles_ref, out_ref, partners_ref, zeros, fetch_sem, sems):
    blocks = out_ref.shape[0]
    fetch = pltpu.make_async_copy(partners_any, partners_ref, fetch_sem)
    fetch.start()
    def copy(b, slot, src):
        return pltpu.make_async_copy(src, out_ref.at[b, slot], sems.at[b * 3 + slot])

    def tile(b, off):
        return tiles_ref.at[pl.ds((b * 3 + off) * HALF, HALF)]

    for b in range(blocks):
        copy(b, 0, tile(b, 0)).start()
    zeros[...] = jnp.zeros_like(zeros)
    fetch.wait()
    for b in range(blocks):
        base = partners_ref[b, 0]
        p1 = partners_ref[b, 1]
        p2 = partners_ref[b, 2]

        @pl.when(p1 == base + 1)
        def _():
            copy(b, 1, tile(b, 1)).start()

        @pl.when(p1 == base + 2)
        def _():
            copy(b, 1, tile(b, 2)).start()

        @pl.when(p1 < 0)
        def _():
            copy(b, 1, zeros).start()

        @pl.when(p2 >= 0)
        def _():
            copy(b, 2, tile(b, 2)).start()

        @pl.when(p2 < 0)
        def _():
            copy(b, 2, zeros).start()

    for b in range(blocks):
        for slot in range(3):
            copy(b, slot, zeros).wait()


def on_device(dosage, partners):
    rows, width = dosage.shape
    samples_total = rows * lax.axis_size("sample")
    blocks = partners.shape[0]
    tiles = blocks * 3
    n_cross = sum(len(tiles_of(start)) for start, _, _, last in PIECES if last == 8)
    n_copies = 6 + n_cross
    dma = pltpu.SemaphoreType.DMA
    sums = pl.pallas_call(
        functools.partial(ld_kernel, lax.axis_size("snp"), samples_total),
        out_shape=pltpu.VMEM((tiles * HALF, BLOCK), F32),
        in_specs=[pl.BlockSpec(memory_space=pl.ANY)],
        out_specs=pl.BlockSpec(memory_space=pltpu.VMEM),
        scratch_shapes=[
            pltpu.VMEM((rows, width), BF16),
            pltpu.VMEM((rows, width), BF16),
            pltpu.VMEM((width, rows), BF16),
            pltpu.VMEM((rows, REACH * BLOCK), BF16),
            pltpu.VMEM((rows, CHUNK), BF16),
            pltpu.VMEM((tiles * BLOCK, BLOCK), F32),
            pltpu.VMEM((tiles * HALF, BLOCK), F32),
            pltpu.VMEM((8, width), F32),
            pltpu.VMEM((8, width), F32),
            pltpu.VMEM((8, width), F32),
            pltpu.VMEM((8, REACH * BLOCK), F32),
            dma,
            dma((2,)),
            dma((2,)),
            dma((len(PIECES),)),
            dma((len(PIECES),)),
            dma((n_copies,)),
            dma((n_copies,)),
        ],
        compiler_params=pltpu.CompilerParams(
            collective_id=0, has_side_effects=True, vmem_limit_bytes=52 * 2**20
        ),
    )(dosage)
    return pl.pallas_call(
        pick_kernel,
        out_shape=jax.ShapeDtypeStruct((blocks, 3, HALF, BLOCK), F32),
        in_specs=[
            pl.BlockSpec(memory_space=pl.ANY),
            pl.BlockSpec(memory_space=pltpu.VMEM),
        ],
        out_specs=pl.BlockSpec(memory_space=pl.ANY),
        scratch_shapes=[
            pltpu.SMEM(partners.shape, jnp.int32),
            pltpu.VMEM((HALF, BLOCK), F32),
            dma,
            dma((tiles,)),
        ],
        compiler_params=pltpu.CompilerParams(vmem_limit_bytes=16 * 2**20),
    )(partners, sums)


def solution(mesh):
    in_specs = (P("sample", ("region", "snp")), P(("region", "snp"), None))
    out_specs = P(("region", "snp"), None, "sample", None)
    return jax.shard_map(
        on_device, mesh=mesh, in_specs=in_specs, out_specs=out_specs, check_vma=False
    )
```
